32 devices in a mesh: grp: 2 (over x), gz: 8 (over z, y), gy: 2 (over core).
Axes of the slice: x: 2, y: 2, z: 4, core: 2. Of those that a mesh axis runs over, the one named last changes fastest.
Arguments:
- density: float32 [256, 64, 1024], P(('grp', 'gz'), 'gy'), parts along dimension 0, may hold values from 0.05 to 17
- bin_exponents: int32 [3], replicated, may hold values from -2 to 2
- writer_table: int32 [3, 8], replicated, may hold values from 0 to 7, each once within a row
Outputs:
- coarse_grid: float32 [32, 8, 128], P(('grp', 'gz'), 'gy'), parts along dimension 0
- finest_coefficients: bfloat16 [16, 2, 8, 65536], P(('grp', 'gz'), 'gy'), parts along dimension 0
- middle_coefficients: bfloat16 [16, 2, 8, 8192], P(('grp', 'gz'), 'gy'), parts along dimension 0
- coarser_coefficients: bfloat16 [16, 2, 8, 1024], P(('grp', 'gz'), 'gy'), parts along dimension 0
The draws below stay inside these ranges and needn't reach their ends.
There are 2 independent parts, one for each index of `grp`. The reference program is written for one: setup_inputs(seed, part) draws one part's arguments, and reference() takes and returns one part's arrays. A program takes and returns all parts, laid end to end along the dimension named above; an argument that names none is the same for every part. Nothing has to cross between parts.
Inputs may be any that keep to these rules, and one draw needn't show every extreme that they name: Each row of writer_table names every writer 0 to 7 once.
All inputs are finite; a program needn't handle non-finite values.
Results may differ from the reference program's by a relative error of at most 0.00115.
Values may be sent and summed in bfloat16 or wider, within the bound.
A program may use at most 128 MiB of HBM per device.

```python
from functools import partial
import jax
import jax.numpy as jnp
from jax import lax

NX = 1024
LEVELS = 3
SWEEPS = 2
NZ = 128
NY = 64
N_GZ = 8
N_GY = 2


def draw_density(key, part):
    key = jax.random.fold_in(key, 11)
    rough_part = jnp.clip(jax.random.normal(key, (NZ, NY, NX), jnp.float32), -4.0, 4.0)
    values = jnp.exp(0.7 * rough_part)
    return values.astype(jnp.float32)


def setup_inputs(seed: int = 0, part: int = 0) -> dict:
    key_list = jax.random.split(jax.random.key(seed), 4)
    part_keys = jax.random.split(jax.random.fold_in(key_list[3], part), 4)
    density = draw_density(jax.random.fold_in(jax.random.fold_in(key_list[3], part), 71), part)
    bin_exponents = jax.random.randint(key_list[1], (LEVELS,), -2, 3).astype(jnp.int32)
    writer_table = jax.vmap(lambda own: jax.random.permutation(own, N_GZ))(jax.random.split(key_list[2], LEVELS)).reshape((LEVELS, N_GZ)).astype(jnp.int32)
    return {"density": density, "bin_exponents": bin_exponents, "writer_table": writer_table}


def upsample(values, dim_index):
    length = values.shape[dim_index] - 1
    lower_part = lax.slice_in_dim(values, 0, length, axis=dim_index)
    upper_part = lax.slice_in_dim(values, 1, length + 1, axis=dim_index)
    middle = (lower_part + upper_part) * 0.5
    stacked = jnp.stack((lower_part, middle), axis=dim_index + 1)
    new_shape = values.shape[:dim_index] + (2 * length,) + values.shape[dim_index + 1:]
    return stacked.reshape(new_shape)


def interpolate(extended):
    widened = jnp.pad(extended, ((0, 0), (0, 0), (0, 1)))
    widened = upsample(widened, 2)
    widened = upsample(widened, 1)
    return upsample(widened, 0)


def restrict(padded, dim_index):
    length = (padded.shape[dim_index] - 4) // 2
    weights = (1.0 / 12.0, 0.5, 5.0 / 6.0, 0.5, 1.0 / 12.0)
    running = lax.slice_in_dim(padded, 0, 2 * length - 1, stride=2, axis=dim_index) * weights[0]
    for offset in range(1, 5):
        shifted = lax.slice_in_dim(padded, offset, offset + 2 * length - 1, stride=2, axis=dim_index)
        running = running + shifted * weights[offset]
    return running


def project_load(padded):
    running = restrict(padded, 2)
    running = restrict(running, 1)
    return restrict(running, 0)


def solve_line(target, dim_index, padder):
    length = target.shape[dim_index]
    iterate = target * 0.75
    for sweep_index in range(SWEEPS):
        padded = padder(iterate)
        lower_part = lax.slice_in_dim(padded, 0, length, axis=dim_index)
        upper_part = lax.slice_in_dim(padded, 2, length + 2, axis=dim_index)
        iterate = (target - (lower_part + upper_part) * (1.0 / 3.0)) * 0.75
    return iterate


def pad_along(values, dim_index):
    widths = [(0, 0), (0, 0), (0, 0)]
    widths[dim_index] = (1, 1)
    return jnp.pad(values, widths)


def inverse_of(row):
    writer_ids = jnp.arange(row.shape[0], dtype=jnp.int32)
    matches = (row[None, :] == writer_ids[:, None]).astype(jnp.int32)
    return jnp.sum(matches * writer_ids[None, :], axis=1).astype(jnp.int32)


def regroup(quantized, row):
    plane_count = quantized.shape[0] // N_GZ
    row_count = quantized.shape[1] // N_GY
    blocks = quantized.reshape(N_GZ, plane_count, N_GY, row_count, quantized.shape[2])
    blocks = blocks.transpose(0, 2, 1, 3, 4).reshape(N_GZ, N_GY, N_GZ, -1)
    return blocks[:, :, inverse_of(row), :].transpose(2, 1, 0, 3)


def reference(density, bin_exponents, writer_table):
    current = density
    outputs = []
    for depth_index in range(LEVELS):
        coarse_nodes = current[::2, ::2, ::2]
        extended = jnp.pad(coarse_nodes, ((0, 1), (0, 1), (0, 0)))
        details = current - interpolate(extended)
        load_term = project_load(jnp.pad(details, 2))
        correction = solve_line(load_term, 2, partial(pad_along, dim_index=2))
        correction = solve_line(correction, 1, partial(pad_along, dim_index=1))
        correction = solve_line(correction, 0, partial(pad_along, dim_index=0))
        current = coarse_nodes + correction
        bin_scale = jnp.exp2(-bin_exponents[depth_index].astype(jnp.float32))
        quantized = (details * bin_scale).astype(jnp.bfloat16)
        outputs.append(regroup(quantized, writer_table[depth_index]))
    return (current, outputs[0], outputs[1], outputs[2])
```

```python
import functools

import jax
import jax.numpy as jnp
import numpy as np
from jax import lax
from jax.experimental import pallas as pl
from jax.experimental.pallas import tpu as pltpu
from jax.sharding import PartitionSpec as P

LEVELS = 3
SWEEPS = 2
BF16 = jnp.bfloat16
F32 = jnp.float32


def line_operator(count):
    half = count // 2
    restrict = np.zeros((half, count))
    for k in range(half):
        for off, weight in zip(range(-2, 3), (1 / 12, 0.5, 5 / 6, 0.5, 1 / 12)):
            if 0 <= 2 * k + off < count:
                restrict[k, 2 * k + off] = weight
    near = np.eye(half, k=1) + np.eye(half, k=-1)
    iterate = 0.75 * restrict
    for _ in range(SWEEPS):
        iterate = 0.75 * (restrict - near @ iterate / 3)
    return iterate


def split_np(value):
    high = value.astype(np.float32).astype(BF16)
    low = (value - high.astype(np.float64)).astype(np.float32).astype(BF16)
    return np.stack([high, low])


def split(value):
    high = value.astype(BF16)
    return high, (value - high.astype(F32)).astype(BF16)


def dot3(left, right):
    (lh, ll), (rh, rl) = left, right
    dot = functools.partial(jnp.dot, preferred_element_type=F32)
    return dot(lh, rh) + dot(ll, rh) + dot(lh, rl)


class Plan:
    def __init__(self, depth, planes, rows, cols, peers):
        self.z, self.y, self.x = planes, rows, cols
        self.zc, self.yc, self.xc = planes // 2, rows // 2, cols // 2
        self.last = depth == LEVELS - 1
        self.kz = self.zc if self.last else self.zc + 1
        self.jy = self.yc if self.last else self.yc + 1
        self.br = 8 if self.last else self.yc + 8
        self.piece = planes * rows // peers
        self.packed = self.piece % 16 == 0
        self.blocks = {}
        total = 0
        for dz in (0, -1, 1, -2, 2):
            ks = [k for k in range(self.kz) if -3 <= k + dz * self.zc <= self.zc + 2]
            if not ks:
                continue
            for dy in (0, 1):
                height = self.br if dy == 0 else 8
                self.blocks[dz, dy] = (total, ks[0], len(ks), height)
                total += len(ks) * height
        self.m = total

    def messages(self):
        return [key for key in self.blocks if key != (0, 0)]

    def rows_matrix(self, peers, side):
        za, ya = line_operator(self.z * peers), line_operator(self.y * side)
        out = []
        for d in (0, peers // 2, peers - 1):
            for e in range(side):
                full = np.zeros((self.m, self.z * self.y))
                for (dz, dy), (start, first, count, height) in self.blocks.items():
                    dest = e if dy == 0 else 1 - e
                    base = 0 if dy == 0 or dest == 1 else self.yc - 3
                    span = self.jy if dy == 0 else (3 if dest == 1 else self.jy - base)
                    for i in range(count):
                        gk = (d + dz) * self.zc + first + i
                        if not 0 <= gk < self.zc * peers:
                            continue
                        zrow = za[gk, d * self.z:(d + 1) * self.z]
                        for j in range(span):
                            gj = dest * self.yc + base + j
                            if gj >= self.yc * side:
                                continue
                            yrow = ya[gj, e * self.y:(e + 1) * self.y]
                            full[start + i * height + j] = np.kron(zrow, yrow)
                out.append(split_np(full))
        return np.stack(out)


def kernel(plans, peers, density, scale, inverse, *refs):
    refs = list(refs)
    take = lambda count: [refs.pop(0) for _ in range(count)]
    row_hbm, col_w, sel_w = take(LEVELS), take(LEVELS), take(LEVELS)
    coarse_out = refs.pop(0)
    outs = take(LEVELS)
    curs, row_w, mids, flats, sends, prods, strips = (take(LEVELS) for _ in range(7))
    slots = [{key: refs.pop(0) for key in plan.messages()} for plan in plans]
    local_sem, rim_send, rim_recv, msg_send, msg_recv, a2a_send, a2a_recv = refs

    g, d, e = lax.axis_index("grp"), lax.axis_index("gz"), lax.axis_index("gy")
    variant = ((d + peers - 1) // peers + d // (peers - 1)) * 2 + e
    plan0 = plans[0]
    nz, ny = plan0.z, plan0.y

    loads = [pltpu.make_async_copy(density, curs[0].at[0:nz, 0:ny], local_sem.at[0])]
    for l in range(LEVELS):
        loads.append(pltpu.make_async_copy(row_hbm[l].at[variant], row_w[l], local_sem.at[1 + l]))
    for load in loads:
        load.start()

    barrier = pltpu.get_barrier_semaphore()
    for s in range(peers):
        for f in range(2):
            if (s, f) != (0, 0):
                pl.semaphore_signal(
                    barrier, inc=1, device_id=(g, lax.rem(d + s, peers), lax.rem(e + f, 2)),
                    device_id_type=pl.DeviceIdType.MESH)
    pl.semaphore_wait(barrier, 2 * peers - 1)

    def remote(src, dst, ssem, rsem, dz, de):
        return pltpu.make_async_remote_copy(
            src_ref=src, dst_ref=dst, send_sem=ssem, recv_sem=rsem,
            device_id=(g, dz, de),
            device_id_type=pl.DeviceIdType.MESH)

    rim = [
        remote(density.at[0], curs[0].at[nz, 0:ny], rim_send.at[0], rim_recv.at[0],
               jnp.maximum(d - 1, 0), e),
        remote(density.at[0, 0:8], curs[0].at[nz, ny:ny + 8], rim_send.at[1], rim_recv.at[1],
               jnp.maximum(d - 1, 0), 0),
        remote(density.at[:, 0:8], curs[0].at[0:nz, ny:ny + 8], rim_send.at[2], rim_recv.at[2],
               d, 0),
    ]
    sends_if = [d > 0, (d > 0) & (e == 1), e == 1]
    recvs_if = [d < peers - 1, (d < peers - 1) & (e == 0), e == 0]
    for copy, cond in zip(rim, sends_if):
        pl.when(cond)(copy.start)

    zero_row = jnp.zeros((nz, 8, plan0.x), F32)
    curs[0][:, ny + 8:ny + 16, :] = jnp.zeros((nz + 1, 8, plan0.x), F32)

    @pl.when(e == 1)
    def _():
        curs[0][0:nz, ny:ny + 8, :] = zero_row
        curs[0][nz, ny:ny + 8, :] = jnp.zeros((8, plan0.x), F32)

    @pl.when((e == 0) & (d == peers - 1))
    def _():
        curs[0][nz, ny:ny + 8, :] = jnp.zeros((8, plan0.x), F32)

    @pl.when(d == peers - 1)
    def _():
        curs[0][nz, 0:ny, :] = jnp.zeros((ny, plan0.x), F32)

    loads[0].wait()
    for copy, cond in zip(rim, recvs_if):
        pl.when(cond)(copy.wait_recv)

    a2a_all = []
    msg_all = []
    for l, plan in enumerate(plans):
        cur, mid, flat, send, prod = curs[l], mids[l], flats[l], sends[l], prods[l]
        z, y, x = plan.z, plan.y, plan.x
        lane = lax.broadcasted_iota(jnp.int32, (y + 8, x), 1)
        row = lax.broadcasted_iota(jnp.int32, (y + 8, x), 0)

        def widen(k, _, cur=cur, mid=mid, y=y, x=x, lane=lane, row=row):
            value = cur[2 * k, 0:y + 8, :]
            after = jnp.where(lane == x - 1, 0.0, pltpu.roll(value, x - 1, 1))
            value = jnp.where(lane % 2 == 1, (pltpu.roll(value, 1, 1) + after) * 0.5, value)
            both = pltpu.roll(value, 1, 0) + pltpu.roll(value, y + 7, 0)
            mid[k] = jnp.where(row % 2 == 1, both * 0.5, value)[0:y]
            return 0

        lax.fori_loop(0, plan.zc + 1, widen, 0)

        factor = scale[l]
        high, low = flat[0], flat[1]

        def subtract(k, _, cur=cur, mid=mid, y=y, high=high, low=low, flat=flat, plan=plan):
            here, there = mid[k], mid[k + 1]
            for odd in range(2):
                inter = (here + there) * 0.5 if odd else here
                detail = cur[2 * k + odd, 0:y, :] - inter
                at = pl.ds(pl.multiple_of((2 * k + odd) * y, y), y)
                quant = detail * factor
                if y % 16 == 0:
                    high[at, :], low[at, :] = split(detail)
                else:
                    high[at, :] = detail
                flat[2][at, :] = quant.astype(flat[2].dtype)
            return 0

        lax.fori_loop(0, plan.zc, subtract, 0)

        height = plan.piece if plan.packed else 8
        cols = lax.broadcasted_iota(jnp.int32, (height, z * y), 1)
        rows = lax.broadcasted_iota(jnp.int32, (height, z * y), 0)
        offset = cols - rows
        if not plan.packed:
            offset = jnp.where(rows < plan.piece, offset, -1)
        order = jnp.concatenate(
            [jnp.where(offset == inverse[l, w] * plan.piece, 1.0, 0.0) for w in range(peers)], axis=0)
        ordered = jnp.dot(order.astype(BF16), flat[2][...].astype(BF16), preferred_element_type=F32)
        send[...] = ordered.reshape(peers, height, x).astype(send.dtype)
        for s in range(1, peers):
            copy = remote(send.at[lax.rem(d + s, peers)], outs[l].at[d], a2a_send.at[l, s],
                          a2a_recv.at[l, s], lax.rem(d + s, peers), e)
            copy.start()
            a2a_all.append(copy)
        outs[l][d] = send[d]

        left = (high[...], low[...]) if y % 16 == 0 else split(high[...])
        inner = dot3(left, (col_w[l][0], col_w[l][1]))
        loads[1 + l].wait()
        prod[...] = dot3((row_w[l][0], row_w[l][1]), split(inner))

        messages = []
        for index, (dz, dy) in enumerate(plan.messages()):
            start, first, count, height = plan.blocks[dz, dy]
            target = jnp.clip(d + dz, 0, peers - 1)
            copy = remote(prod.at[start:start + count * height], slots[l][dz, dy],
                          msg_send.at[l, index], msg_recv.at[l, index],
                          target, e if dy == 0 else 1 - e)
            goes = (d + dz >= 0) & (d + dz < peers)
            comes = (d - dz >= 0) & (d - dz < peers)
            if dz == 0:
                copy.start()
            else:
                pl.when(goes)(copy.start)
            messages.append((copy, goes, comes, dz, dy))
        msg_all.extend(messages)

        br = plan.br
        target_ref = coarse_out if plan.last else curs[l + 1]
        strip = strips[l]
        for k in range(plan.kz):
            for b in range(x // 128):
                strip[b, k * 2 * br:(k + 1) * 2 * br, :] = cur[2 * k, 0:2 * br, b * 128:(b + 1) * 128]
        nodes = jnp.concatenate(
            [strip[b, pl.ds(0, plan.kz * br, stride=2), :] for b in range(x // 128)], axis=1)
        nh, nl = split(nodes)
        sel = sel_w[l][...]
        picked = (jnp.dot(nh, sel, preferred_element_type=F32)
                  + jnp.dot(nl, sel, preferred_element_type=F32))
        start = plan.blocks[0, 0][0]
        picked = picked + prod[start:start + plan.kz * br, :]
        for k in range(plan.kz):
            target_ref[k, 0:br, :] = picked[k * br:(k + 1) * br]
            if not plan.last:
                target_ref[k, br:br + 8, :] = jnp.zeros((8, plan.xc), F32)
        for copy, goes, comes, dz, dy in messages:
            _, first, count, height = plan.blocks[dz, dy]

            def add(copy=copy, dz=dz, dy=dy, first=first, count=count, height=height, l=l, plan=plan,
                    target_ref=target_ref):
                copy.wait_recv()
                slot = slots[l][dz, dy]
                for i in range(count):
                    got = slot[i * height:(i + 1) * height, :]
                    if dy == 0:
                        target_ref[first + i, 0:height, :] = target_ref[first + i, 0:height, :] + got
                    else:
                        low_row, span = plan.yc - 3, plan.jy - plan.yc + 3

                        @pl.when(e == 0)
                        def _():
                            target_ref[first + i, low_row:low_row + span, :] = (
                                target_ref[first + i, low_row:low_row + span, :] + got[0:span])

                        @pl.when(e == 1)
                        def _():
                            target_ref[first + i, 0:3, :] = target_ref[first + i, 0:3, :] + got[0:3]

            if dz == 0:
                add()
            else:
                pl.when(comes)(add)

    for copy, cond in zip(rim, sends_if):
        pl.when(cond)(copy.wait_send)
    for copy, goes, comes, dz, dy in msg_all:
        if dz == 0:
            copy.wait_send()
        else:
            pl.when(goes)(copy.wait_send)
    for copy in a2a_all:
        copy.wait()


def inverse_of(table):
    ids = jnp.arange(table.shape[1], dtype=jnp.int32)
    matches = (table[:, None, :] == ids[None, :, None]).astype(jnp.int32)
    return jnp.sum(matches * ids[None, None, :], axis=2)


def shards(density, bin_exponents, writer_table):
    peers, side = lax.axis_size("gz"), lax.axis_size("gy")
    nz, ny, nx = density.shape
    plans = [Plan(l, nz >> l, ny >> l, nx >> l, peers) for l in range(LEVELS)]
    row_w = [jnp.asarray(plan.rows_matrix(peers, side)) for plan in plans]
    col_w = [jnp.asarray(split_np(line_operator(plan.x).T)) for plan in plans]
    sel_w = [jnp.asarray(np.eye(plan.x)[:, ::2].astype(BF16)) for plan in plans]
    bin_scale = jnp.exp2(-bin_exponents.astype(F32))

    out_shape = [jax.ShapeDtypeStruct((plans[-1].zc, 8, plans[-1].xc), F32)]
    for plan in plans:
        if plan.packed:
            out_shape.append(jax.ShapeDtypeStruct((peers, plan.piece, plan.x), BF16))
        else:
            out_shape.append(jax.ShapeDtypeStruct((peers, 8, plan.x), F32))

    scratch = []
    scratch += [pltpu.VMEM((p.z + 1, p.y + 16, p.x), F32) for p in plans]
    scratch += [pltpu.VMEM((2, p.m, p.z * p.y), BF16) for p in plans]
    scratch += [pltpu.VMEM((p.zc + 1, p.y, p.x), F32) for p in plans]
    for p in plans:
        scratch.append([pltpu.VMEM((p.z * p.y, p.x), BF16 if p.y % 16 == 0 else F32)] * 3)
    for shape in out_shape[1:]:
        scratch.append(pltpu.VMEM(shape.shape, shape.dtype))
    scratch += [pltpu.VMEM((p.m, p.xc), F32) for p in plans]
    scratch += [pltpu.VMEM((p.x // 128, p.kz * 2 * p.br, 128), F32) for p in plans]
    for p in plans:
        for key in p.messages():
            _, _, count, height = p.blocks[key]
            scratch.append(pltpu.VMEM((count * height, p.xc), F32))
    most = max(len(p.messages()) for p in plans)
    scratch += [pltpu.SemaphoreType.DMA((1 + LEVELS,))]
    scratch += [pltpu.SemaphoreType.DMA((3,))] * 2
    scratch += [pltpu.SemaphoreType.DMA((LEVELS, most))] * 2
    scratch += [pltpu.SemaphoreType.DMA((LEVELS, peers))] * 2

    vmem, smem, hbm = (pl.BlockSpec(memory_space=s) for s in (pltpu.VMEM, pltpu.SMEM, pl.ANY))
    outputs = pl.pallas_call(
        functools.partial(kernel, plans, peers),
        out_shape=out_shape,
        in_specs=[hbm, smem, smem] + [hbm] * LEVELS + [vmem] * (2 * LEVELS),
        out_specs=[vmem] * (1 + LEVELS),
        scratch_shapes=scratch,
        compiler_params=pltpu.CompilerParams(
            collective_id=0, has_side_effects=True, vmem_limit_bytes=56 * 1024 * 1024),
        cost_estimate=pl.CostEstimate(flops=10**9, bytes_accessed=10**7, transcendentals=0),
    )(density, bin_scale, inverse_of(writer_table), *row_w, *col_w, *sel_w)
    coarse = outputs[0][:, 0:plans[-1].yc, :]
    results = [coarse]
    for plan, value in zip(plans, outputs[1:]):
        if not plan.packed:
            value = value[:, 0:plan.piece, :].astype(BF16)
        results.append(value.reshape(1, 1, peers, -1))
    return tuple(results)


def solution(mesh):
    in_specs = (P(("grp", "gz"), "gy", None), P(), P())
    out_specs = (
        P(("grp", "gz"), "gy", None),
        P(("grp", "gz"), "gy", None, None),
        P(("grp", "gz"), "gy", None, None),
        P(("grp", "gz"), "gy", None, None),
    )
    return jax.shard_map(shards, mesh=mesh, in_specs=in_specs, out_specs=out_specs, check_vma=False)
```

```python
import functools

import jax
import jax.numpy as jnp
import numpy as np
from jax import lax
from jax.experimental import pallas as pl
from jax.experimental.pallas import tpu as pltpu
from jax.sharding import PartitionSpec as P

LEVELS = 3
SWEEPS = 2
BF16 = jnp.bfloat16
F32 = jnp.float32


def line_operator(count):
    half = count // 2
    restrict = np.zeros((half, count))
    for k in range(half):
        for off, weight in zip(range(-2, 3), (1 / 12, 0.5, 5 / 6, 0.5, 1 / 12)):
            if 0 <= 2 * k + off < count:
                restrict[k, 2 * k + off] = weight
    near = np.eye(half, k=1) + np.eye(half, k=-1)
    iterate = 0.75 * restrict
    for _ in range(SWEEPS):
        iterate = 0.75 * (restrict - near @ iterate / 3)
    return iterate


def split_np(value):
    high = value.astype(np.float32).astype(BF16)
    low = (value - high.astype(np.float64)).astype(np.float32).astype(BF16)
    return np.stack([high, low])


def split(value):
    high = value.astype(BF16)
    return high, (value - high.astype(F32)).astype(BF16)


def dot3(left, right):
    (lh, ll), (rh, rl) = left, right
    dot = functools.partial(jnp.dot, preferred_element_type=F32)
    return dot(lh, rh) + dot(ll, rh) + dot(lh, rl)


class Plan:
    def __init__(self, depth, planes, rows, cols, peers):
        self.z, self.y, self.x = planes, rows, cols
        self.zc, self.yc, self.xc = planes // 2, rows // 2, cols // 2
        self.last = depth == LEVELS - 1
        self.kz = self.zc if self.last else self.zc + 1
        self.jy = self.yc if self.last else self.yc + 1
        self.br = 8 if self.last else self.yc + 8
        self.piece = planes * rows // peers
        self.packed = self.piece % 16 == 0
        self.blocks = {}
        total = 0
        for dz in (0, -1, 1, -2, 2):
            ks = [k for k in range(self.kz) if -3 <= k + dz * self.zc <= self.zc + 2]
            if not ks:
                continue
            for dy in (0, 1):
                height = self.br if dy == 0 else 8
                self.blocks[dz, dy] = (total, ks[0], len(ks), height)
                total += len(ks) * height
        self.m = total

    def messages(self):
        return [key for key in self.blocks if key != (0, 0)]

    def rows_matrix(self, peers, side):
        za, ya = line_operator(self.z * peers), line_operator(self.y * side)
        out = []
        for d in (0, peers // 2, peers - 1):
            for e in range(side):
                full = np.zeros((self.m, self.z * self.y))
                for (dz, dy), (start, first, count, height) in self.blocks.items():
                    dest = e if dy == 0 else 1 - e
                    base = 0 if dy == 0 or dest == 1 else self.yc - 3
                    span = self.jy if dy == 0 else (3 if dest == 1 else self.jy - base)
                    for i in range(count):
                        gk = (d + dz) * self.zc + first + i
                        if not 0 <= gk < self.zc * peers:
                            continue
                        zrow = za[gk, d * self.z:(d + 1) * self.z]
                        for j in range(span):
                            gj = dest * self.yc + base + j
                            if gj >= self.yc * side:
                                continue
                            yrow = ya[gj, e * self.y:(e + 1) * self.y]
                            full[start + i * height + j] = np.kron(zrow, yrow)
                out.append(split_np(full))
        return np.stack(out)


def kernel(plans, peers, density, exponents, table, *refs):
    refs = list(refs)
    take = lambda count: [refs.pop(0) for _ in range(count)]
    row_hbm, col_hbm, sel_hbm = take(LEVELS), take(LEVELS), take(LEVELS)
    coarse_out = refs.pop(0)
    outs = take(LEVELS)
    curs, row_w, mids, flats, sends, prods, strips, col_w, sel_w, gathers = (take(LEVELS) for _ in range(10))
    slots = [{key: refs.pop(0) for key in plan.messages()} for plan in plans]
    coarse_full, local_sem, rim_send, rim_recv, msg_send, msg_recv, a2a_send, a2a_recv = refs

    g, d, e = lax.axis_index("grp"), lax.axis_index("gz"), lax.axis_index("gy")
    def inverse(l, w):
        return sum(jnp.where(table[l, p] == w, p, 0) for p in range(peers))

    variant = ((d + peers - 1) // peers + d // (peers - 1)) * 2 + e
    plan0 = plans[0]
    nz, ny = plan0.z, plan0.y

    loads = [pltpu.make_async_copy(density, curs[0].at[0:nz, 0:ny], local_sem.at[0])]
    for l in range(LEVELS):
        loads.append(pltpu.make_async_copy(row_hbm[l].at[variant], row_w[l], local_sem.at[1 + 3 * l]))
        loads.append(pltpu.make_async_copy(col_hbm[l], col_w[l], local_sem.at[2 + 3 * l]))
        loads.append(pltpu.make_async_copy(sel_hbm[l], sel_w[l], local_sem.at[3 + 3 * l]))
    for load in loads:
        load.start()

    barrier = pltpu.get_barrier_semaphore()
    for s in range(peers):
        for f in range(2):
            if (s, f) != (0, 0):
                pl.semaphore_signal(
                    barrier, inc=1, device_id=(g, lax.rem(d + s, peers), lax.rem(e + f, 2)),
                    device_id_type=pl.DeviceIdType.MESH)
    pl.semaphore_wait(barrier, 2 * peers - 1)

    def remote(src, dst, ssem, rsem, dz, de):
        return pltpu.make_async_remote_copy(
            src_ref=src, dst_ref=dst, send_sem=ssem, recv_sem=rsem,
            device_id=(g, dz, de),
            device_id_type=pl.DeviceIdType.MESH)

    rim = [
        remote(density.at[0], curs[0].at[nz, 0:ny], rim_send.at[0], rim_recv.at[0],
               jnp.maximum(d - 1, 0), e),
        remote(density.at[0, 0:8], curs[0].at[nz, ny:ny + 8], rim_send.at[1], rim_recv.at[1],
               jnp.maximum(d - 1, 0), 0),
        remote(density.at[:, 0:8], curs[0].at[0:nz, ny:ny + 8], rim_send.at[2], rim_recv.at[2],
               d, 0),
    ]
    sends_if = [d > 0, (d > 0) & (e == 1), e == 1]
    recvs_if = [d < peers - 1, (d < peers - 1) & (e == 0), e == 0]
    for copy, cond in zip(rim, sends_if):
        pl.when(cond)(copy.start)

    zero_row = jnp.zeros((nz, 8, plan0.x), F32)
    curs[0][:, ny + 8:ny + 16, :] = jnp.zeros((nz + 1, 8, plan0.x), F32)

    @pl.when(e == 1)
    def _():
        curs[0][0:nz, ny:ny + 8, :] = zero_row
        curs[0][nz, ny:ny + 8, :] = jnp.zeros((8, plan0.x), F32)

    @pl.when((e == 0) & (d == peers - 1))
    def _():
        curs[0][nz, ny:ny + 8, :] = jnp.zeros((8, plan0.x), F32)

    @pl.when(d == peers - 1)
    def _():
        curs[0][nz, 0:ny, :] = jnp.zeros((ny, plan0.x), F32)

    loads[0].wait()
    pl.when(recvs_if[2])(rim[2].wait_recv)

    a2a_all = [[] for _ in range(LEVELS)]
    msg_all = []
    for l, plan in enumerate(plans):
        cur, mid, flat, send, prod = curs[l], mids[l], flats[l], sends[l], prods[l]
        z, y, x = plan.z, plan.y, plan.x
        lane = lax.broadcasted_iota(jnp.int32, (y + 8, x), 1)
        row = lax.broadcasted_iota(jnp.int32, (y + 8, x), 0)

        def widen(k, _, cur=cur, mid=mid, y=y, x=x, lane=lane, row=row):
            value = cur[2 * k, 0:y + 8, :]
            after = jnp.where(lane == x - 1, 0.0, pltpu.roll(value, x - 1, 1))
            value = jnp.where(lane % 2 == 1, (pltpu.roll(value, 1, 1) + after) * 0.5, value)
            both = pltpu.roll(value, 1, 0) + pltpu.roll(value, y + 7, 0)
            mid[k] = jnp.where(row % 2 == 1, both * 0.5, value)[0:y]
            return 0

        lax.fori_loop(0, plan.zc, widen, 0)
        if l > 0:
            widen(plan.zc, 0)

        factor = jnp.float32(1.0)
        for power in range(-4, 5):
            factor = jnp.where(exponents[l] == power, 2.0 ** -power, factor)
        high, low = flat[0], flat[1]

        def subtract(k, _, cur=cur, mid=mid, y=y, high=high, low=low, flat=flat, plan=plan):
            here, there = mid[k], mid[k + 1]
            for odd in range(2):
                inter = (here + there) * 0.5 if odd else here
                detail = cur[2 * k + odd, 0:y, :] - inter
                at = pl.ds(pl.multiple_of((2 * k + odd) * y, y), y)
                quant = detail * factor
                if y % 16 == 0:
                    high[at, :], low[at, :] = split(detail)
                else:
                    high[at, :] = detail
                flat[2][at, :] = quant.astype(flat[2].dtype)
            return 0

        if l > 0:
            lax.fori_loop(0, plan.zc, subtract, 0)
        else:
            lax.fori_loop(0, plan.zc - 1, subtract, 0)
            pl.when(recvs_if[0])(rim[0].wait_recv)
            pl.when(recvs_if[1])(rim[1].wait_recv)
            widen(plan.zc, 0)
            subtract(plan.zc - 1, 0)

        height = plan.piece if plan.packed else 8
        cols = lax.broadcasted_iota(jnp.int32, (height, z * y), 1)
        rows = lax.broadcasted_iota(jnp.int32, (height, z * y), 0)
        offset = cols - rows
        if not plan.packed:
            offset = jnp.where(rows < plan.piece, offset, -1)
        order = jnp.concatenate(
            [jnp.where(offset == inverse(l, w) * plan.piece, 1.0, 0.0) for w in range(peers)], axis=0)
        ordered = jnp.dot(order.astype(BF16), flat[2][...].astype(BF16), preferred_element_type=F32)
        send[...] = ordered.reshape(peers, height, x).astype(send.dtype)
        for s in range(1, peers):
            copy = remote(send.at[lax.rem(d + s, peers)], gathers[l].at[d], a2a_send.at[l, s],
                          a2a_recv.at[l, s], lax.rem(d + s, peers), e)
            copy.start()
            a2a_all[l].append(copy)
        gathers[l][d] = send[d]

        for load in loads[1 + 3 * l:4 + 3 * l]:
            load.wait()
        left = (high[...], low[...]) if y % 16 == 0 else split(high[...])
        inner = dot3(left, (col_w[l][0], col_w[l][1]))
        prod[...] = dot3((row_w[l][0], row_w[l][1]), split(inner))

        messages = []
        for index, (dz, dy) in enumerate(plan.messages()):
            start, first, count, height = plan.blocks[dz, dy]
            target = jnp.clip(d + dz, 0, peers - 1)
            copy = remote(prod.at[start:start + count * height], slots[l][dz, dy],
                          msg_send.at[l, index], msg_recv.at[l, index],
                          target, e if dy == 0 else 1 - e)
            goes = (d + dz >= 0) & (d + dz < peers)
            comes = (d - dz >= 0) & (d - dz < peers)
            if dz == 0:
                copy.start()
            else:
                pl.when(goes)(copy.start)
            messages.append((copy, goes, comes, dz, dy))
        msg_all.extend(messages)

        br = plan.br
        target_ref = coarse_full if plan.last else curs[l + 1]
        strip = strips[l]
        for k in range(plan.kz):
            for b in range(x // 128):
                strip[b, k * 2 * br:(k + 1) * 2 * br, :] = cur[2 * k, 0:2 * br, b * 128:(b + 1) * 128]
        nodes = jnp.concatenate(
            [strip[b, pl.ds(0, plan.kz * br, stride=2), :] for b in range(x // 128)], axis=1)
        nh, nl = split(nodes)
        sel = sel_w[l][...]
        picked = (jnp.dot(nh, sel, preferred_element_type=F32)
                  + jnp.dot(nl, sel, preferred_element_type=F32))
        start = plan.blocks[0, 0][0]
        picked = picked + prod[start:start + plan.kz * br, :]
        for k in range(plan.kz):
            target_ref[k, 0:br, :] = picked[k * br:(k + 1) * br]
            if not plan.last:
                target_ref[k, br:br + 8, :] = jnp.zeros((8, plan.xc), F32)
        for copy, goes, comes, dz, dy in messages:
            _, first, count, height = plan.blocks[dz, dy]

            def add(copy=copy, dz=dz, dy=dy, first=first, count=count, height=height, l=l, plan=plan,
                    target_ref=target_ref):
                copy.wait_recv()
                slot = slots[l][dz, dy]
                for i in range(count):
                    got = slot[i * height:(i + 1) * height, :]
                    if dy == 0:
                        target_ref[first + i, 0:height, :] = target_ref[first + i, 0:height, :] + got
                    else:
                        low_row, span = plan.yc - 3, plan.jy - plan.yc + 3

                        @pl.when(e == 0)
                        def _():
                            target_ref[first + i, low_row:low_row + span, :] = (
                                target_ref[first + i, low_row:low_row + span, :] + got[0:span])

                        @pl.when(e == 1)
                        def _():
                            target_ref[first + i, 0:3, :] = target_ref[first + i, 0:3, :] + got[0:3]

            if dz == 0:
                add()
            else:
                pl.when(comes)(add)

    for copy, cond in zip(rim, sends_if):
        pl.when(cond)(copy.wait_send)
    for copy, goes, comes, dz, dy in msg_all:
        if dz == 0:
            copy.wait_send()
        else:
            pl.when(goes)(copy.wait_send)
    coarse_out[...] = coarse_full[:, 0:plans[-1].yc, :]

    for l in reversed(range(LEVELS)):
        for copy in a2a_all[l]:
            copy.wait()
        plan = plans[l]
        height = plan.piece if plan.packed else 8
        count = plan.piece * peers
        to = lax.broadcasted_iota(jnp.int32, (count, peers * height), 0)
        at = lax.broadcasted_iota(jnp.int32, (count, peers * height), 1)
        turn = jnp.where(at == to % peers * height + to // peers, 1.0, 0.0).astype(BF16)
        turned = jnp.dot(turn, gathers[l][...].reshape(peers * height, plan.x).astype(BF16),
                         preferred_element_type=F32).astype(BF16)
        for r in range(plan.piece):
            outs[l][0, 0, :, r * plan.x:(r + 1) * plan.x] = turned[r * peers:(r + 1) * peers]


def shards(density, bin_exponents, writer_table):
    peers, side = lax.axis_size("gz"), lax.axis_size("gy")
    nz, ny, nx = density.shape
    plans = [Plan(l, nz >> l, ny >> l, nx >> l, peers) for l in range(LEVELS)]
    row_w = [jnp.asarray(plan.rows_matrix(peers, side)) for plan in plans]
    col_w = [jnp.asarray(split_np(line_operator(plan.x).T)) for plan in plans]
    sel_w = [jnp.asarray(np.eye(plan.x)[:, ::2].astype(BF16)) for plan in plans]

    out_shape = [jax.ShapeDtypeStruct((plans[-1].zc, plans[-1].yc, plans[-1].xc), F32)]
    for plan in plans:
        out_shape.append(jax.ShapeDtypeStruct((1, 1, peers, plan.piece * plan.x), BF16))

    scratch = []
    scratch += [pltpu.VMEM((p.z + 1, p.y + 16, p.x), F32) for p in plans]
    scratch += [pltpu.VMEM((2, p.m, p.z * p.y), BF16) for p in plans]
    scratch += [pltpu.VMEM((p.zc + 1, p.y, p.x), F32) for p in plans]
    for p in plans:
        scratch.append([pltpu.VMEM((p.z * p.y, p.x), BF16 if p.y % 16 == 0 else F32)] * 3)
    scratch += [pltpu.VMEM((peers, p.piece if p.packed else 8, p.x), BF16 if p.packed else F32)
                for p in plans]
    scratch += [pltpu.VMEM((p.m, p.xc), F32) for p in plans]
    scratch += [pltpu.VMEM((p.x // 128, p.kz * 2 * p.br, 128), F32) for p in plans]
    scratch += [pltpu.VMEM((2, p.x, p.xc), BF16) for p in plans]
    scratch += [pltpu.VMEM((p.x, p.xc), BF16) for p in plans]
    scratch += [pltpu.VMEM((peers, p.piece if p.packed else 8, p.x), BF16 if p.packed else F32)
                for p in plans]
    for p in plans:
        for key in p.messages():
            _, _, count, height = p.blocks[key]
            scratch.append(pltpu.VMEM((count * height, p.xc), F32))
    most = max(len(p.messages()) for p in plans)
    scratch.append(pltpu.VMEM((plans[-1].zc, 8, plans[-1].xc), F32))
    scratch += [pltpu.SemaphoreType.DMA((1 + 3 * LEVELS,))]
    scratch += [pltpu.SemaphoreType.DMA((3,))] * 2
    scratch += [pltpu.SemaphoreType.DMA((LEVELS, most))] * 2
    scratch += [pltpu.SemaphoreType.DMA((LEVELS, peers))] * 2

    vmem, smem, hbm = (pl.BlockSpec(memory_space=s) for s in (pltpu.VMEM, pltpu.SMEM, pl.ANY))
    return tuple(pl.pallas_call(
        functools.partial(kernel, plans, peers),
        out_shape=out_shape,
        in_specs=[hbm, smem, smem] + [hbm] * (3 * LEVELS),
        out_specs=[vmem] * (1 + LEVELS),
        scratch_shapes=scratch,
        compiler_params=pltpu.CompilerParams(
            collective_id=0, has_side_effects=True, vmem_limit_bytes=56 * 1024 * 1024),
        cost_estimate=pl.CostEstimate(flops=10**9, bytes_accessed=10**7, transcendentals=0),
    )(density, bin_exponents, writer_table, *row_w, *col_w, *sel_w))


def solution(mesh):
    in_specs = (P(("grp", "gz"), "gy", None), P(), P())
    out_specs = (
        P(("grp", "gz"), "gy", None),
        P(("grp", "gz"), "gy", None, None),
        P(("grp", "gz"), "gy", None, None),
        P(("grp", "gz"), "gy", None, None),
    )
    return jax.shard_map(shards, mesh=mesh, in_specs=in_specs, out_specs=out_specs, check_vma=False)
```

```python
import functools

import jax
import jax.numpy as jnp
import numpy as np
from jax import lax
from jax.experimental import pallas as pl
from jax.experimental.pallas import tpu as pltpu
from jax.sharding import PartitionSpec as P

LEVELS = 3
SWEEPS = 2
BF16 = jnp.bfloat16
F32 = jnp.float32


def line_operator(count):
    half = count // 2
    restrict = np.zeros((half, count))
    for k in range(half):
        for off, weight in zip(range(-2, 3), (1 / 12, 0.5, 5 / 6, 0.5, 1 / 12)):
            if 0 <= 2 * k + off < count:
                restrict[k, 2 * k + off] = weight
    near = np.eye(half, k=1) + np.eye(half, k=-1)
    iterate = 0.75 * restrict
    for _ in range(SWEEPS):
        iterate = 0.75 * (restrict - near @ iterate / 3)
    return iterate


def split_np(value):
    high = value.astype(np.float32).astype(BF16)
    low = (value - high.astype(np.float64)).astype(np.float32).astype(BF16)
    return np.stack([high, low])


def split(value):
    high = value.astype(BF16)
    return high, (value - high.astype(F32)).astype(BF16)


def dot3(left, right):
    (lh, ll), (rh, rl) = left, right
    dot = functools.partial(jnp.dot, preferred_element_type=F32)
    return dot(lh, rh) + dot(ll, rh) + dot(lh, rl)


class Plan:
    def __init__(self, depth, planes, rows, cols, peers):
        self.z, self.y, self.x = planes, rows, cols
        self.zc, self.yc, self.xc = planes // 2, rows // 2, cols // 2
        self.last = depth == LEVELS - 1
        self.kz = self.zc if self.last else self.zc + 1
        self.jy = self.yc if self.last else self.yc + 1
        self.br = 8 if self.last else self.yc + 8
        self.piece = planes * rows // peers
        self.packed = self.piece % 16 == 0
        self.blocks = {}
        total = 0
        for dz in (0, -1, 1, -2, 2):
            ks = [k for k in range(self.kz) if -3 <= k + dz * self.zc <= self.zc + 2]
            if not ks:
                continue
            for dy in (0, 1):
                if dy == 1:
                    height, size = 4, -(-len(ks) * 4 // 8) * 8
                elif dz == 0 or self.last:
                    height, size = self.br, len(ks) * self.br
                else:
                    height, size = self.yc, len(ks) * self.yc + 8
                self.blocks[dz, dy] = (total, ks[0], len(ks), height, size)
                total += size
        self.m = total

    def messages(self):
        return [key for key in self.blocks if key != (0, 0)]

    def rows_matrix(self, peers, side):
        za, ya = line_operator(self.z * peers), line_operator(self.y * side)
        out = []
        for d in (0, peers // 2, peers - 1):
            for e in range(side):
                full = np.zeros((self.m, self.z * self.y))
                for (dz, dy), (start, first, count, height, _) in self.blocks.items():
                    dest = e if dy == 0 else 1 - e
                    base = 0 if dy == 0 or dest == 1 else self.yc - 3
                    span = self.jy if dy == 0 else (3 if dest == 1 else self.jy - base)
                    for i in range(count):
                        gk = (d + dz) * self.zc + first + i
                        if not 0 <= gk < self.zc * peers:
                            continue
                        zrow = za[gk, d * self.z:(d + 1) * self.z]
                        for j in range(span):
                            gj = dest * self.yc + base + j
                            if gj >= self.yc * side:
                                continue
                            yrow = ya[gj, e * self.y:(e + 1) * self.y]
                            at = start + i * height + j
                            if dy == 0 and dz != 0 and j >= height:
                                at = start + count * height + i
                            full[at] = np.kron(zrow, yrow)
                out.append(split_np(full))
        return np.stack(out)


def kernel(plans, peers, density, paired, exponents, table, *refs):
    refs = list(refs)
    take = lambda count: [refs.pop(0) for _ in range(count)]
    row_hbm, col_hbm, sel_hbm = take(LEVELS), take(LEVELS), take(LEVELS)
    coarse_out = refs.pop(0)
    outs = take(LEVELS)
    curs, row_w, mids, flats, sends, prods, strips, col_w, sel_w, gathers = (take(LEVELS) for _ in range(10))
    slots = [{key: refs.pop(0) for key in plan.messages()} for plan in plans]
    coarse_full, row_rim, local_sem, rim_send, rim_recv, msg_send, msg_recv, a2a_send, a2a_recv = refs

    g, d, e = lax.axis_index("grp"), lax.axis_index("gz"), lax.axis_index("gy")
    def inverse(l, w):
        return sum(jnp.where(table[l, p] == w, p, 0) for p in range(peers))

    variant = ((d + peers - 1) // peers + d // (peers - 1)) * 2 + e
    plan0 = plans[0]
    nz, ny = plan0.z, plan0.y

    loads = [pltpu.make_async_copy(density, curs[0].at[0:nz, 0:ny], local_sem.at[0])]
    for l in range(LEVELS):
        loads.append(pltpu.make_async_copy(row_hbm[l].at[variant], row_w[l], local_sem.at[1 + 3 * l]))
        loads.append(pltpu.make_async_copy(col_hbm[l], col_w[l], local_sem.at[2 + 3 * l]))
        loads.append(pltpu.make_async_copy(sel_hbm[l], sel_w[l], local_sem.at[3 + 3 * l]))
    for load in loads:
        load.start()

    barrier = pltpu.get_barrier_semaphore()
    for s in range(peers):
        for f in range(2):
            if (s, f) != (0, 0):
                pl.semaphore_signal(
                    barrier, inc=1, device_id=(g, lax.rem(d + s, peers), lax.rem(e + f, 2)),
                    device_id_type=pl.DeviceIdType.MESH)
    pl.semaphore_wait(barrier, 2 * peers - 1)

    def remote(src, dst, ssem, rsem, dz, de):
        return pltpu.make_async_remote_copy(
            src_ref=src, dst_ref=dst, send_sem=ssem, recv_sem=rsem,
            device_id=(g, dz, de),
            device_id_type=pl.DeviceIdType.MESH)

    rim = [
        remote(density.at[0], curs[0].at[nz, 0:ny], rim_send.at[0], rim_recv.at[0],
               jnp.maximum(d - 1, 0), e),
        remote(density.at[0, 0:8], curs[0].at[nz, ny:ny + 8], rim_send.at[1], rim_recv.at[1],
               jnp.maximum(d - 1, 0), 0),
        remote(paired.at[:, 0, 0:8], row_rim, rim_send.at[2], rim_recv.at[2],
               d, 0),
    ]
    sends_if = [d > 0, (d > 0) & (e == 1), e == 1]
    recvs_if = [d < peers - 1, (d < peers - 1) & (e == 0), e == 0]
    for copy, cond in zip(rim, sends_if):
        pl.when(cond)(copy.start)

    zero_row = jnp.zeros((nz, 8, plan0.x), F32)
    curs[0][:, ny + 8:ny + 16, :] = jnp.zeros((nz + 1, 8, plan0.x), F32)

    @pl.when(e == 1)
    def _():
        curs[0][0:nz, ny:ny + 8, :] = zero_row
        curs[0][nz, ny:ny + 8, :] = jnp.zeros((8, plan0.x), F32)

    @pl.when((e == 0) & (d == peers - 1))
    def _():
        curs[0][nz, ny:ny + 8, :] = jnp.zeros((8, plan0.x), F32)

    @pl.when(d == peers - 1)
    def _():
        curs[0][nz, 0:ny, :] = jnp.zeros((ny, plan0.x), F32)

    loads[0].wait()
    @pl.when(recvs_if[2])
    def _():
        rim[2].wait_recv()
        for k in range(nz // 2):
            curs[0][2 * k, ny:ny + 8, :] = row_rim[k]


    a2a_all = [[] for _ in range(LEVELS)]
    msg_all = []
    far_first = sorted(range(1, peers), key=lambda s: abs(2 * s - peers))
    for l, plan in enumerate(plans):
        cur, mid, flat, send, prod = curs[l], mids[l], flats[l], sends[l], prods[l]
        z, y, x = plan.z, plan.y, plan.x
        lane = lax.broadcasted_iota(jnp.int32, (y + 8, x), 1)
        row = lax.broadcasted_iota(jnp.int32, (y + 8, x), 0)

        def widen(k, _, cur=cur, mid=mid, y=y, x=x, lane=lane, row=row):
            value = cur[2 * k, 0:y + 8, :]
            after = jnp.where(lane == x - 1, 0.0, pltpu.roll(value, x - 1, 1))
            value = jnp.where(lane % 2 == 1, (pltpu.roll(value, 1, 1) + after) * 0.5, value)
            both = pltpu.roll(value, 1, 0) + pltpu.roll(value, y + 7, 0)
            mid[k] = jnp.where(row % 2 == 1, both * 0.5, value)[0:y]
            return 0

        lax.fori_loop(0, plan.zc, widen, 0)
        if l > 0:
            widen(plan.zc, 0)

        factor = jnp.float32(1.0)
        for power in range(-4, 5):
            factor = jnp.where(exponents[l] == power, 2.0 ** -power, factor)
        high, low = flat[0], flat[1]

        def subtract(k, _, cur=cur, mid=mid, y=y, high=high, low=low, flat=flat, plan=plan):
            here, there = mid[k], mid[k + 1]
            for odd in range(2):
                inter = (here + there) * 0.5 if odd else here
                detail = cur[2 * k + odd, 0:y, :] - inter
                at = pl.ds(pl.multiple_of((2 * k + odd) * y, y), y)
                quant = detail * factor
                if y % 16 == 0:
                    high[at, :], low[at, :] = split(detail)
                else:
                    high[at, :] = detail
                flat[2][at, :] = quant.astype(flat[2].dtype)
            return 0

        if l > 0:
            lax.fori_loop(0, plan.zc, subtract, 0)
        else:
            lax.fori_loop(0, plan.zc - 1, subtract, 0)
            pl.when(recvs_if[0])(rim[0].wait_recv)
            pl.when(recvs_if[1])(rim[1].wait_recv)
            widen(plan.zc, 0)
            subtract(plan.zc - 1, 0)

        height = plan.piece if plan.packed else 8
        cols = lax.broadcasted_iota(jnp.int32, (height, z * y), 1)
        rows = lax.broadcasted_iota(jnp.int32, (height, z * y), 0)
        offset = cols - rows
        if not plan.packed:
            offset = jnp.where(rows < plan.piece, offset, -1)
        order = jnp.concatenate(
            [jnp.where(offset == inverse(l, w) * plan.piece, 1.0, 0.0) for w in range(peers)], axis=0)
        ordered = jnp.dot(order.astype(BF16), flat[2][...].astype(BF16), preferred_element_type=F32)
        send[...] = ordered.reshape(peers, height, x).astype(send.dtype)
        for s in range(1, peers):
            copy = remote(send.at[lax.rem(d + s, peers)], gathers[l].at[d], a2a_send.at[l, s],
                          a2a_recv.at[l, s], lax.rem(d + s, peers), e)
            a2a_all[l].append(copy)
        gathers[l][d] = send[d]

        for load in loads[1 + 3 * l:4 + 3 * l]:
            load.wait()
        left = (high[...], low[...]) if y % 16 == 0 else split(high[...])
        inner = dot3(left, (col_w[l][0], col_w[l][1]))
        prod[...] = dot3((row_w[l][0], row_w[l][1]), split(inner))

        messages = []
        for index, (dz, dy) in enumerate(plan.messages()):
            start, size = plan.blocks[dz, dy][0], plan.blocks[dz, dy][4]
            target = jnp.clip(d + dz, 0, peers - 1)
            copy = remote(prod.at[start:start + size], slots[l][dz, dy],
                          msg_send.at[l, index], msg_recv.at[l, index],
                          target, e if dy == 0 else 1 - e)
            goes = (d + dz >= 0) & (d + dz < peers)
            comes = (d - dz >= 0) & (d - dz < peers)
            if dz == 0:
                copy.start()
            else:
                pl.when(goes)(copy.start)
            messages.append((copy, goes, comes, dz, dy))
        msg_all.extend(messages)
        if l > 0:
            for copy in a2a_all[l]:
                copy.start()
        for index in range(l, peers - 1, LEVELS):
            a2a_all[0][far_first[index] - 1].start()

        br = plan.br
        target_ref = coarse_full if plan.last else curs[l + 1]
        strip = strips[l]
        for k in range(plan.kz):
            for b in range(x // 128):
                strip[b, k * 2 * br:(k + 1) * 2 * br, :] = cur[2 * k, 0:2 * br, b * 128:(b + 1) * 128]
        nodes = jnp.concatenate(
            [strip[b, pl.ds(0, plan.kz * br, stride=2), :] for b in range(x // 128)], axis=1)
        nh, nl = split(nodes)
        sel = sel_w[l][...]
        picked = (jnp.dot(nh, sel, preferred_element_type=F32)
                  + jnp.dot(nl, sel, preferred_element_type=F32))
        start = plan.blocks[0, 0][0]
        picked = picked + prod[start:start + plan.kz * br, :]
        for k in range(plan.kz):
            target_ref[k, 0:br, :] = picked[k * br:(k + 1) * br]
            if not plan.last:
                target_ref[k, br:br + 8, :] = jnp.zeros((8, plan.xc), F32)
        for copy, goes, comes, dz, dy in messages:
            _, first, count, height, _ = plan.blocks[dz, dy]

            def add(copy=copy, dz=dz, dy=dy, first=first, count=count, height=height, l=l, plan=plan,
                    target_ref=target_ref):
                copy.wait_recv()
                slot = slots[l][dz, dy]
                for i in range(count):
                    got = slot[i * height:(i + 1) * height, :]
                    if dy == 0:
                        target_ref[first + i, 0:height, :] = target_ref[first + i, 0:height, :] + got
                        if dz != 0 and not plan.last:
                            edge, at = plan.yc, count * height + i
                            target_ref[first + i, edge:edge + 1, :] = (
                                target_ref[first + i, edge:edge + 1, :] + slot[at:at + 1, :])
                    else:
                        low_row, span = plan.yc - 3, plan.jy - plan.yc + 3

                        @pl.when(e == 0)
                        def _():
                            target_ref[first + i, low_row:low_row + span, :] = (
                                target_ref[first + i, low_row:low_row + span, :] + got[0:span])

                        @pl.when(e == 1)
                        def _():
                            target_ref[first + i, 0:3, :] = target_ref[first + i, 0:3, :] + got[0:3]

            if dz == 0:
                add()
            else:
                pl.when(comes)(add)

    for copy, cond in zip(rim, sends_if):
        pl.when(cond)(copy.wait_send)
    for copy, goes, comes, dz, dy in msg_all:
        if dz == 0:
            copy.wait_send()
        else:
            pl.when(goes)(copy.wait_send)
    coarse_out[...] = coarse_full[:, 0:plans[-1].yc, :]

    for l in reversed(range(LEVELS)):
        for copy in a2a_all[l]:
            copy.wait()
        plan = plans[l]
        height = plan.piece if plan.packed else 8
        count = plan.piece * peers
        to = lax.broadcasted_iota(jnp.int32, (count, peers * height), 0)
        at = lax.broadcasted_iota(jnp.int32, (count, peers * height), 1)
        turn = jnp.where(at == to % peers * height + to // peers, 1.0, 0.0).astype(BF16)
        turned = jnp.dot(turn, gathers[l][...].reshape(peers * height, plan.x).astype(BF16),
                         preferred_element_type=F32).astype(BF16)
        for r in range(plan.piece):
            outs[l][0, 0, :, r * plan.x:(r + 1) * plan.x] = turned[r * peers:(r + 1) * peers]


def shards(density, bin_exponents, writer_table):
    peers, side = lax.axis_size("gz"), lax.axis_size("gy")
    nz, ny, nx = density.shape
    plans = [Plan(l, nz >> l, ny >> l, nx >> l, peers) for l in range(LEVELS)]
    row_w = [jnp.asarray(plan.rows_matrix(peers, side)) for plan in plans]
    col_w = [jnp.asarray(split_np(line_operator(plan.x).T)) for plan in plans]
    sel_w = [jnp.asarray(np.eye(plan.x)[:, ::2].astype(BF16)) for plan in plans]

    out_shape = [jax.ShapeDtypeStruct((plans[-1].zc, plans[-1].yc, plans[-1].xc), F32)]
    for plan in plans:
        out_shape.append(jax.ShapeDtypeStruct((1, 1, peers, plan.piece * plan.x), BF16))

    scratch = []
    scratch += [pltpu.VMEM((p.z + 1, p.y + 16, p.x), F32) for p in plans]
    scratch += [pltpu.VMEM((2, p.m, p.z * p.y), BF16) for p in plans]
    scratch += [pltpu.VMEM((p.zc + 1, p.y, p.x), F32) for p in plans]
    for p in plans:
        scratch.append([pltpu.VMEM((p.z * p.y, p.x), BF16 if p.y % 16 == 0 else F32)] * 3)
    scratch += [pltpu.VMEM((peers, p.piece if p.packed else 8, p.x), BF16 if p.packed else F32)
                for p in plans]
    scratch += [pltpu.VMEM((p.m, p.xc), F32) for p in plans]
    scratch += [pltpu.VMEM((p.x // 128, p.kz * 2 * p.br, 128), F32) for p in plans]
    scratch += [pltpu.VMEM((2, p.x, p.xc), BF16) for p in plans]
    scratch += [pltpu.VMEM((p.x, p.xc), BF16) for p in plans]
    scratch += [pltpu.VMEM((peers, p.piece if p.packed else 8, p.x), BF16 if p.packed else F32)
                for p in plans]
    for p in plans:
        for key in p.messages():
            scratch.append(pltpu.VMEM((p.blocks[key][4], p.xc), F32))
    most = max(len(p.messages()) for p in plans)
    scratch.append(pltpu.VMEM((plans[-1].zc, 8, plans[-1].xc), F32))
    scratch.append(pltpu.VMEM((nz // 2, 8, nx), F32))
    scratch += [pltpu.SemaphoreType.DMA((1 + 3 * LEVELS,))]
    scratch += [pltpu.SemaphoreType.DMA((3,))] * 2
    scratch += [pltpu.SemaphoreType.DMA((LEVELS, most))] * 2
    scratch += [pltpu.SemaphoreType.DMA((LEVELS, peers))] * 2

    vmem, smem, hbm = (pl.BlockSpec(memory_space=s) for s in (pltpu.VMEM, pltpu.SMEM, pl.ANY))
    return tuple(pl.pallas_call(
        functools.partial(kernel, plans, peers),
        out_shape=out_shape,
        in_specs=[hbm, hbm, smem, smem] + [hbm] * (3 * LEVELS),
        out_specs=[vmem] * (1 + LEVELS),
        scratch_shapes=scratch,
        compiler_params=pltpu.CompilerParams(
            collective_id=0, has_side_effects=True, vmem_limit_bytes=56 * 1024 * 1024),
        cost_estimate=pl.CostEstimate(flops=10**9, bytes_accessed=10**7, transcendentals=0),
    )(density, density.reshape(nz // 2, 2, ny, nx), bin_exponents, writer_table, *row_w, *col_w, *sel_w))


def solution(mesh):
    in_specs = (P(("grp", "gz"), "gy", None), P(), P())
    out_specs = (
        P(("grp", "gz"), "gy", None),
        P(("grp", "gz"), "gy", None, None),
        P(("grp", "gz"), "gy", None, None),
        P(("grp", "gz"), "gy", None, None),
    )
    return jax.shard_map(shards, mesh=mesh, in_specs=in_specs, out_specs=out_specs, check_vma=False)
```
